32 devices in a mesh: groups: 2 (over y), rows: 8 (over z, core), cols: 2 (over x).
Axes of the slice: x: 2, y: 2, z: 4, core: 2. Of those that a mesh axis runs over, the one named last changes fastest.
Arguments:
- tile_values: bfloat16 [16, 2, 384, 128, 128], P(('groups', 'rows'), 'cols'), parts along dimension 0, may hold values from 0.049804688 to 5
- sketch: bfloat16 [32768, 256], P(('groups', 'rows', 'cols')), parts along dimension 0, may hold values from -6 to 6
- tile_coords: int32 [16, 2, 2, 384], P(('groups', 'rows'), 'cols'), parts along dimension 0, may hold values from 0 to 63, as said below
- tile_counts: int32 [16, 2], P(('groups', 'rows'), 'cols'), parts along dimension 0, may hold values from 1 to 384, as said below
Outputs:
- range_basis: float32 [32768, 256], P(('groups', 'cols', 'rows')), parts along dimension 0
The draws below stay inside these ranges and needn't reach their ends.
There are 2 independent parts, one for each index of `groups`. The reference program is written for one: setup_inputs(seed, part) draws one part's arguments, and reference() takes and returns one part's arrays. A program takes and returns all parts, laid end to end along the dimension named above; each array names one. Nothing has to cross between parts.
Inputs may be any that keep to these rules, and one draw needn't show every extreme that they name: `tile_coords`: the live positions of one device are distinct; every tile on the diagonal of the matrix is live; row numbers are below 64 and column numbers below 16. `tile_counts`: at most 384 live slots a device, reached by some device in every draw.
All inputs are finite; a program needn't handle non-finite values.
Results may differ from the reference program's by a relative error of at most 0.0003.
Values may be sent and summed in bfloat16 or wider, within the bound.
A program may use at most 64 MiB of HBM per device.

```python
import math
import jax
import jax.numpy as jnp
from jax import lax

TILE_SIZE = 128
SKETCH = 256
COL_TILES = 16
STATES = 16384
SLOTS = 384
N_ROWS = 8
N_COLS = 2


def tile_layout(key):
    first, second, third = jax.random.split(jax.random.fold_in(key, 11), 3)
    row_tiles = COL_TILES * N_ROWS // N_COLS
    places = row_tiles * COL_TILES
    position = jnp.arange(places, dtype=jnp.int32)
    place_row = position // COL_TILES
    place_col = position % COL_TILES
    col_block = jnp.arange(N_ROWS, dtype=jnp.int32)[:, None, None]
    row_block = jnp.arange(N_COLS, dtype=jnp.int32)[None, :, None]
    on_diagonal = row_block * row_tiles + place_row[None, None, :] == col_block * COL_TILES + place_col[None, None, :]
    on_diagonal = on_diagonal.astype(jnp.int32)
    scores = jax.random.randint(first, (N_ROWS, N_COLS, places), 0, 65536) * places + position[None, None, :]
    scores = scores + on_diagonal * (65536 * places)
    _, chosen = lax.top_k(scores, SLOTS)
    coords = jnp.stack([place_row[chosen], place_col[chosen]], axis=2).astype(jnp.int32)
    needed = jnp.sum(on_diagonal, axis=2)
    counts = jax.random.randint(second, (N_ROWS, N_COLS), SLOTS // 4, SLOTS // 2 + 1)
    counts = jnp.maximum(jnp.maximum(counts, needed), 1)
    picked = jax.random.randint(third, (), 0, N_ROWS * N_COLS)
    flat_index = jnp.arange(N_ROWS * N_COLS, dtype=jnp.int32).reshape(N_ROWS, N_COLS)
    counts = jnp.where(flat_index == picked, SLOTS, counts).astype(jnp.int32)
    return (coords, counts)


def draw_tile_coords(key, part):
    return tile_layout(key)[0]


def draw_tile_counts(key, part):
    return tile_layout(key)[1]


def block_levels(rng, shape, shards, low, largest):
    gain, own = 1.0, jax.random.fold_in(rng, 6)
    for dim, blocks in shards:
        draws = jnp.exp(jax.random.uniform(jax.random.fold_in(own, dim), (blocks,), jnp.float32, low / len(shards), largest / len(shards)))
        gain = gain * jnp.repeat(draws, shape[dim] // blocks).reshape([-1 if axis == dim else 1 for axis in range(len(shape))])
    return gain


def gaussian(rng, shape, scale, most, shards=(), held_as=jnp.bfloat16):
    entries = scale * jax.random.normal(rng, shape, jnp.float32)
    if shards:
        entries = entries * block_levels(rng, shape, shards, -0.22, 0.18)
    return jnp.clip(entries, -most, most).astype(held_as)


def setup_inputs(seed: int = 0, part: int = 0) -> dict:
    key_of = jax.random.split(jax.random.key(seed), 5)
    own_keys = jax.random.split(jax.random.fold_in(key_of[4], part), 5)
    tile_values = jnp.clip(jnp.exp(math.log(5.0) - 4.609084 * jax.random.uniform(own_keys[0], (N_ROWS, N_COLS, SLOTS, TILE_SIZE, TILE_SIZE), jnp.float32) ** block_levels(own_keys[0], (N_ROWS, N_COLS, SLOTS, TILE_SIZE, TILE_SIZE), ((0, 8), (1, 2)), -0.2, 0.2)), 0.049804688, 5.0).astype(jnp.bfloat16)
    sketch = gaussian(own_keys[1], (STATES, SKETCH), 1.0, 6.0, ((0, 16),))
    tile_coords = draw_tile_coords(jax.random.fold_in(jax.random.fold_in(key_of[4], part), 71), part)
    tile_counts = draw_tile_counts(jax.random.fold_in(jax.random.fold_in(key_of[4], part), 71), part)
    return {"tile_values": tile_values, "sketch": sketch, "tile_coords": tile_coords, "tile_counts": tile_counts}


def reference(tile_values, sketch, tile_coords, tile_counts):
    row_tiles = COL_TILES * N_ROWS // N_COLS
    states = TILE_SIZE * COL_TILES * N_ROWS
    sketch_tiles = sketch.astype(jnp.float32).reshape(states // TILE_SIZE, TILE_SIZE, SKETCH)
    slot_index = jnp.arange(SLOTS, dtype=jnp.int32)

    def visit(carry, device):
        products, totals = carry
        col_block = device // N_COLS
        row_block = device % N_COLS
        values = tile_values[col_block, row_block].astype(jnp.float32)
        coords = tile_coords[col_block, row_block]
        live = tile_counts[col_block, row_block]
        global_rows = (row_block * row_tiles + coords[0]).astype(jnp.int32)
        global_cols = (col_block * COL_TILES + coords[1]).astype(jnp.int32)
        weight = (slot_index < live).astype(jnp.float32)
        gathered = sketch_tiles[global_cols]
        terms = jnp.einsum('bij,bjk->bik', values, gathered) * weight[:, None, None]
        sums = lax.optimization_barrier(jnp.sum(values, axis=2)) * weight[:, None]
        return ((products.at[global_rows].add(terms), totals.at[global_rows].add(sums)), None)
    start = (jnp.zeros((states // TILE_SIZE, TILE_SIZE, SKETCH), jnp.float32), jnp.zeros((states // TILE_SIZE, TILE_SIZE), jnp.float32))
    (products, totals), _ = lax.scan(visit, start, jnp.arange(N_ROWS * N_COLS, dtype=jnp.int32))
    image = (products / totals[:, :, None]).reshape(states, SKETCH)
    factor_q, factor_r = jnp.linalg.qr(image)
    signs = jnp.sign(jnp.diagonal(factor_r))
    return factor_q * signs[None, :] * jnp.sqrt(jnp.float32(states))
```

```python
import functools
import math

import jax
import jax.numpy as jnp
from jax import lax
from jax.experimental import pallas as pl
from jax.experimental.pallas import tpu as pltpu
from jax.sharding import PartitionSpec as P

TILE_SIZE = 128
SKETCH = 256
MESH = pl.DeviceIdType.MESH
CHUNKS = 3
EXTRA = 8
PANEL = 32
HIGHEST = lax.Precision.HIGHEST


def spread(n_rows, n_cols, slots, share, col_tiles, map_ref, tiles_hbm, sketch_hbm, image_ref, gram_ref,
           tiles, block, pair, own, sib_out, sib_in, from_left, from_right,
           tile_sem, local_sem, sk_send, sk_recv, sib_send, sib_recv,
           right_send, right_recv, left_send, left_recv):
    length = n_rows // 2
    part = block.shape[0] // n_cols
    pairs = share // 256
    rows = (share + EXTRA) // CHUNKS
    me = lax.axis_index("rows")
    col = lax.axis_index("cols")
    z = me // 2
    core = lax.rem(me, 2)
    sibling = z * 2 + 1 - core

    tile_copy = pltpu.make_async_copy(tiles_hbm, tiles.at[pl.ds(0, slots)], tile_sem)
    tile_copy.start()
    mine = pl.ds(pl.multiple_of(col * part, part), part)
    sketch_copy = pltpu.make_async_copy(sketch_hbm, block.at[mine], local_sem)
    sketch_copy.start()

    barrier = pltpu.get_barrier_semaphore()
    pl.semaphore_signal(barrier, inc=1, device_id={"rows": sibling}, device_id_type=MESH)
    for step in range(1, n_cols):
        peer = lax.rem(col + step, n_cols)
        pl.semaphore_signal(barrier, inc=1, device_id={"cols": peer}, device_id_type=MESH)

    @pl.when(z > 0)
    def _():
        pl.semaphore_signal(barrier, inc=1, device_id={"rows": me - 2}, device_id_type=MESH)

    @pl.when(z < length - 1)
    def _():
        pl.semaphore_signal(barrier, inc=1, device_id={"rows": me + 2}, device_id_type=MESH)

    near = jnp.where(z > 0, 1, 0) + jnp.where(z < length - 1, 1, 0)
    pl.semaphore_wait(barrier, n_cols + near)

    def sketch_send(step):
        peer = lax.rem(col + step, n_cols)
        return pltpu.make_async_remote_copy(
            src_ref=sketch_hbm, dst_ref=block.at[mine], send_sem=sk_send.at[step], recv_sem=sk_recv.at[step],
            device_id={"cols": peer}, device_id_type=MESH)

    for step in range(1, n_cols):
        sketch_send(step).start()
    tiles[slots] = jnp.zeros((TILE_SIZE, TILE_SIZE), jnp.bfloat16)
    tile_copy.wait()
    sketch_copy.wait()
    for step in range(1, n_cols):
        sketch_send(step).wait()

    ones = jnp.ones((EXTRA, TILE_SIZE), jnp.float32)
    extra_id = lax.broadcasted_iota(jnp.int32, (EXTRA, TILE_SIZE), 0)

    def partial(number, dst, where):
        dst[where, pl.ds(share, EXTRA), :] = jnp.zeros((EXTRA, SKETCH), jnp.float32)

        def one(index, carry):
            for half in range(2):
                base = ((number * pairs + index) * 2 + half) * col_tiles
                total = jnp.zeros((TILE_SIZE, TILE_SIZE), jnp.float32)
                for c in range(col_tiles):
                    slab = tiles[map_ref[base + c]]
                    pair[half * TILE_SIZE:(half + 1) * TILE_SIZE, c * TILE_SIZE:(c + 1) * TILE_SIZE] = slab
                    total = total + slab.astype(jnp.float32)
                sums = lax.dot_general(ones, total, (((1,), (1,)), ((), ())), precision=HIGHEST,
                                       preferred_element_type=jnp.float32)
                lanes = slice(half * TILE_SIZE, (half + 1) * TILE_SIZE)
                kept = dst[where, pl.ds(share, EXTRA), lanes]
                dst[where, pl.ds(share, EXTRA), lanes] = jnp.where(extra_id == index, sums, kept)
            dst[where, pl.ds(pl.multiple_of(index * 256, 256), 256), :] = jnp.dot(
                pair[...], block[...], preferred_element_type=jnp.float32)
            return carry

        lax.fori_loop(0, pairs, one, 0)

    def sib_copy(d):
        return pltpu.make_async_remote_copy(
            src_ref=sib_out.at[d], dst_ref=sib_in.at[d], send_sem=sib_send.at[d], recv_sem=sib_recv.at[d],
            device_id={"rows": sibling}, device_id_type=MESH)

    def right_copy(source, d, c):
        return pltpu.make_async_remote_copy(
            src_ref=source.at[d, pl.ds(c * rows, rows)], dst_ref=from_left.at[d, pl.ds(c * rows, rows)],
            send_sem=right_send.at[d, c], recv_sem=right_recv.at[d, c],
            device_id={"rows": me + 2}, device_id_type=MESH)

    def left_copy(source, d, c):
        return pltpu.make_async_remote_copy(
            src_ref=source.at[d, pl.ds(c * rows, rows)], dst_ref=from_right.at[d, pl.ds(c * rows, rows)],
            send_sem=left_send.at[d, c], recv_sem=left_recv.at[d, c],
            device_id={"rows": me - 2}, device_id_type=MESH)

    def visit(p, carry):
        half = p // 2
        d = jnp.where(lax.rem(p, 2) == 0, length - 1 - half, half)
        partial(d * 2 + 1 - core, sib_out, d)
        sib_copy(d).start()
        partial(d * 2 + core, own, d)
        sib_copy(d).wait()
        own[d] = own[d] + sib_in[d]

        @pl.when((z == 0) & (d > 0))
        def _():
            for c in range(CHUNKS):
                right_copy(own, d, c).start()

        @pl.when((z == length - 1) & (d < z))
        def _():
            for c in range(CHUNKS):
                left_copy(own, d, c).start()

        return carry

    lax.fori_loop(0, length, visit, 0)

    def forward(s, carry):
        d = length - 1 - s
        e = s
        for c in range(CHUNKS):
            span = pl.ds(c * rows, rows)

            @pl.when((z > 0) & (d >= z))
            def _():
                right_copy(from_left, d, c).wait_recv()

                @pl.when(d > z)
                def _():
                    from_left[d, span] = from_left[d, span] + own[d, span]
                    right_copy(from_left, d, c).start()

                @pl.when(d == z)
                def _():
                    own[d, span] = own[d, span] + from_left[d, span]

            @pl.when((z < length - 1) & (e <= z))
            def _():
                left_copy(from_right, e, c).wait_recv()

                @pl.when(e < z)
                def _():
                    from_right[e, span] = from_right[e, span] + own[e, span]
                    left_copy(from_right, e, c).start()

                @pl.when(e == z)
                def _():
                    own[e, span] = own[e, span] + from_right[e, span]

        return carry

    lax.fori_loop(0, length, forward, 0)

    eye = lax.broadcasted_iota(jnp.int32, (256, 256), 0) == lax.broadcasted_iota(jnp.int32, (256, 256), 1)
    gram_ref[...] = jnp.zeros_like(gram_ref)

    def finish(index, carry):
        extra = own[z, pl.ds(share, EXTRA), :]
        picked = lax.broadcasted_iota(jnp.int32, (EXTRA, SKETCH), 0) == index
        line = jnp.sum(jnp.where(picked, extra, 0.0), axis=0, keepdims=True)
        totals = jnp.sum(jnp.where(eye, jnp.broadcast_to(line, (256, 256)), 0.0), axis=1, keepdims=True)
        where = pl.ds(pl.multiple_of(index * 256, 256), 256)
        image = own[z, where, :] / totals
        image_ref[where, :] = image
        gram_ref[...] += lax.dot_general(image, image, (((0,), (0,)), ((), ())), precision=HIGHEST,
                                         preferred_element_type=jnp.float32)
        return carry

    lax.fori_loop(0, pairs, finish, 0)

    def settle(d, carry):
        for c in range(CHUNKS):
            @pl.when((z < length - 1) & (d > z))
            def _():
                right_copy(own, d, c).wait_send()

            @pl.when((z > 0) & (d < z))
            def _():
                left_copy(own, d, c).wait_send()
        return carry

    lax.fori_loop(0, length, settle, 0)


def factor(scale, gram_ref, image_ref, out_ref, work):
    size = SKETCH
    work[:, :size] = gram_ref[...]
    work[:, size:] = (lax.broadcasted_iota(jnp.int32, (size, size), 0)
                      == lax.broadcasted_iota(jnp.int32, (size, size), 1)).astype(jnp.float32)
    row_id = lax.broadcasted_iota(jnp.int32, (PANEL, 1), 0)
    for k in range(size // PANEL):
        first = k * PANEL
        panel = work[first:first + PANEL, :]
        for j in range(PANEL):
            at = first + j
            column = panel[:, at:at + 1]
            inverse = lax.rsqrt(panel[j:j + 1, at:at + 1])
            line = panel[j:j + 1, :] * inverse
            weight = jnp.where(row_id > j, column * inverse, 0.0)
            panel = jnp.where(row_id == j, line, panel - weight * line)
        work[first:first + PANEL, :] = panel
        after = first + PANEL
        if after < size:
            work[after:, :] -= lax.dot_general(
                panel[:, :size], panel, (((0,), (0,)), ((), ())), precision=HIGHEST,
                preferred_element_type=jnp.float32)[after:, :]
    lower = work[:, size:] * scale
    out_ref[...] = lax.dot_general(image_ref[...], lower, (((1,), (1,)), ((), ())), precision=HIGHEST,
                                   preferred_element_type=jnp.float32)


def per_device(tile_values, sketch, tile_coords, tile_counts):
    n_rows = lax.axis_size("rows")
    n_cols = lax.axis_size("cols")
    slots = tile_values.shape[2]
    depth = sketch.shape[0] * n_cols
    col_tiles = depth // TILE_SIZE
    row_tiles = col_tiles * n_rows // n_cols
    share = row_tiles * TILE_SIZE // n_rows
    length = n_rows // 2
    slot = jnp.arange(slots, dtype=jnp.int32)
    place = jnp.where(slot < tile_counts[0, 0], tile_coords[0, 0, 0] * col_tiles + tile_coords[0, 0, 1], -1)
    places = jnp.arange(row_tiles * col_tiles, dtype=jnp.int32)
    where = jnp.min(jnp.where(places[:, None] == place[None, :], slot[None, :], slots), axis=1)
    f32, vmem = jnp.float32, pltpu.VMEM
    dma = pltpu.SemaphoreType.DMA
    image, gram = pl.pallas_call(
        functools.partial(spread, n_rows, n_cols, slots, share, col_tiles),
        out_shape=(jax.ShapeDtypeStruct((share, SKETCH), f32), jax.ShapeDtypeStruct((SKETCH, SKETCH), f32)),
        in_specs=[pl.BlockSpec(memory_space=pltpu.SMEM), pl.BlockSpec(memory_space=pl.ANY),
                  pl.BlockSpec(memory_space=pl.ANY)],
        out_specs=(pl.BlockSpec(memory_space=vmem), pl.BlockSpec(memory_space=vmem)),
        scratch_shapes=[
            vmem((slots + 1, TILE_SIZE, TILE_SIZE), jnp.bfloat16),
            vmem((depth, SKETCH), jnp.bfloat16),
            vmem((256, depth), jnp.bfloat16),
        ] + [vmem((length, share + EXTRA, SKETCH), f32)] * 5 + [
            dma, dma, dma((n_cols,)), dma((n_cols,)), dma((length,)), dma((length,)),
        ] + [dma((length, CHUNKS))] * 4,
        compiler_params=pltpu.CompilerParams(collective_id=0, has_side_effects=True,
                                             vmem_limit_bytes=56 * 1024 * 1024),
    )(where, tile_values.reshape(slots, TILE_SIZE, TILE_SIZE), sketch)
    gram = lax.psum(gram, ("rows", "cols"))
    scale = math.sqrt(float(row_tiles * TILE_SIZE * n_cols))
    return pl.pallas_call(
        functools.partial(factor, scale),
        out_shape=jax.ShapeDtypeStruct((share, SKETCH), f32),
        in_specs=[pl.BlockSpec(memory_space=vmem)] * 2,
        out_specs=pl.BlockSpec(memory_space=vmem),
        scratch_shapes=[vmem((SKETCH, 2 * SKETCH), f32)],
        compiler_params=pltpu.CompilerParams(vmem_limit_bytes=32 * 1024 * 1024),
    )(gram, image)


def solution(mesh):
    return jax.shard_map(
        per_device,
        mesh=mesh,
        in_specs=(
            P(("groups", "rows"), "cols", None, None, None),
            P(("groups", "rows", "cols"), None),
            P(("groups", "rows"), "cols", None, None),
            P(("groups", "rows"), "cols"),
        ),
        out_specs=P(("groups", "cols", "rows"), None),
        check_vma=False,
    )
```

```python
import functools
import math

import jax
import jax.numpy as jnp
from jax import lax
from jax.experimental import pallas as pl
from jax.experimental.pallas import tpu as pltpu
from jax.sharding import PartitionSpec as P

TILE_SIZE = 128
SKETCH = 256
MESH = pl.DeviceIdType.MESH
EXTRA = 8
PANEL = 32
HIGHEST = lax.Precision.HIGHEST


def aligned(number, unit):
    return number * unit if isinstance(number, int) else pl.multiple_of(number * unit, unit)


def spread(n_rows, n_cols, slots, share, col_tiles, map_ref, tiles_hbm, sketch_hbm, image_ref, gram_ref,
           tiles, block, pair, own, sib_out, sib_in, code_out, code_left, code_right, side_out, side_left, side_right,
           gram, gram_sib, gram_half, gram_z, gram_cols, gram_all,
           tile_sem, local_sem, sk_send, sk_recv, sib_send, sib_recv,
           right_send, right_recv, left_send, left_recv,
           half_sem, sum_send, sum_recv, col_send, col_recv, back_send, back_recv):
    length = n_rows // 2
    part = block.shape[0] // n_cols
    pairs = share // 256
    piece = 128 // length
    me = lax.axis_index("rows")
    col = lax.axis_index("cols")
    z = me // 2
    core = lax.rem(me, 2)
    sibling = z * 2 + 1 - core

    tile_copy = pltpu.make_async_copy(tiles_hbm, tiles.at[pl.ds(0, slots)], tile_sem)
    tile_copy.start()
    mine = pl.ds(pl.multiple_of(col * part, part), part)
    sketch_copy = pltpu.make_async_copy(sketch_hbm, block.at[mine], local_sem)
    sketch_copy.start()

    barrier = pltpu.get_barrier_semaphore()
    pl.semaphore_signal(barrier, inc=1, device_id={"rows": sibling}, device_id_type=MESH)
    for step in range(1, n_cols):
        peer = lax.rem(col + step, n_cols)
        pl.semaphore_signal(barrier, inc=1, device_id={"cols": peer}, device_id_type=MESH)

    for step in range(1, length):
        peer = lax.rem(z + step, length) * 2 + core
        pl.semaphore_signal(barrier, inc=1, device_id={"rows": peer}, device_id_type=MESH)
    pl.semaphore_wait(barrier, n_cols + length - 1)

    def sketch_send(step):
        peer = lax.rem(col + step, n_cols)
        return pltpu.make_async_remote_copy(
            src_ref=sketch_hbm, dst_ref=block.at[mine], send_sem=sk_send.at[step], recv_sem=sk_recv.at[step],
            device_id={"cols": peer}, device_id_type=MESH)

    for step in range(1, n_cols):
        sketch_send(step).start()
    tiles[slots] = jnp.zeros((TILE_SIZE, TILE_SIZE), jnp.bfloat16)
    tile_copy.wait()
    sketch_copy.wait()
    for step in range(1, n_cols):
        sketch_send(step).wait()

    ones = jnp.ones((EXTRA, TILE_SIZE), jnp.float32)
    extra_id = lax.broadcasted_iota(jnp.int32, (EXTRA, TILE_SIZE), 0)

    def partial(number, dst, where):
        dst[where, pl.ds(share, EXTRA), :] = jnp.zeros((EXTRA, SKETCH), jnp.float32)

        def one(index, carry):
            for half in range(2):
                base = ((number * pairs + index) * 2 + half) * col_tiles
                total = jnp.zeros((TILE_SIZE, TILE_SIZE), jnp.float32)
                for c in range(col_tiles):
                    slab = tiles[map_ref[base + c]]
                    pair[half * TILE_SIZE:(half + 1) * TILE_SIZE, c * TILE_SIZE:(c + 1) * TILE_SIZE] = slab
                    total = total + slab.astype(jnp.float32)
                sums = lax.dot_general(ones, total, (((1,), (1,)), ((), ())), precision=HIGHEST,
                                       preferred_element_type=jnp.float32)
                lanes = slice(half * TILE_SIZE, (half + 1) * TILE_SIZE)
                kept = dst[where, pl.ds(share, EXTRA), lanes]
                dst[where, pl.ds(share, EXTRA), lanes] = jnp.where(extra_id == index, sums, kept)
            dst[where, pl.ds(pl.multiple_of(index * 256, 256), 256), :] = jnp.dot(
                pair[...], block[...], preferred_element_type=jnp.float32)
            return carry

        lax.fori_loop(0, pairs, one, 0)

    def sib_copy(d):
        return pltpu.make_async_remote_copy(
            src_ref=sib_out.at[d], dst_ref=sib_in.at[d], send_sem=sib_send.at[d], recv_sem=sib_recv.at[d],
            device_id={"rows": sibling}, device_id_type=MESH)

    def chain_copies(to_right, d, c):
        rows, lines = pl.ds(aligned(c, 256), 256), pl.ds(aligned(c, 8), 8)
        code, side = (code_left, side_left) if to_right else (code_right, side_right)
        send, recv = (right_send, right_recv) if to_right else (left_send, left_recv)
        peer = me + 2 if to_right else me - 2
        return (
            pltpu.make_async_remote_copy(
                src_ref=code_out.at[d, rows], dst_ref=code.at[d, rows], send_sem=send.at[d, c, 0],
                recv_sem=recv.at[d, c, 0], device_id={"rows": peer}, device_id_type=MESH),
            pltpu.make_async_remote_copy(
                src_ref=side_out.at[d, lines], dst_ref=side.at[d, lines], send_sem=send.at[d, c, 1],
                recv_sem=recv.at[d, c, 1], device_id={"rows": peer}, device_id_type=MESH),
        )

    eye = lax.broadcasted_iota(jnp.int32, (256, 256), 0) == lax.broadcasted_iota(jnp.int32, (256, 256), 1)
    line_id = lax.broadcasted_iota(jnp.int32, (EXTRA, SKETCH), 0)

    def upright(line):
        return jnp.sum(jnp.where(eye, jnp.broadcast_to(line, (256, 256)), 0.0), axis=1, keepdims=True)

    def totals_line(d, c):
        return jnp.sum(jnp.where(line_id == c, own[d, pl.ds(share, EXTRA), :], 0.0), axis=0, keepdims=True)

    def emit(to_right, d, c):
        rows = pl.ds(aligned(c, 256), 256)
        line = totals_line(d, c)
        ratio = own[d, rows, :] / upright(jnp.where(line > 0, line, 1.0))
        step = jnp.maximum(jnp.max(jnp.abs(ratio), axis=0, keepdims=True) * (1.0 / 32767.0), 1e-30)
        code_out[d, rows, :] = jnp.round(ratio * (1.0 / step)).astype(jnp.int32).astype(jnp.int16)
        side_out[d, pl.ds(aligned(c, 8), 8), :] = jnp.where(line_id == 0, line, step)
        for copy in chain_copies(to_right, d, c):
            copy.start()

    def absorb(to_right, d, c):
        for copy in chain_copies(to_right, d, c):
            copy.wait_recv()
        code, side = (code_left, side_left) if to_right else (code_right, side_right)
        rows, extra = pl.ds(aligned(c, 256), 256), pl.ds(share, EXTRA)
        lines = side[d, pl.ds(aligned(c, 8), 8), :]
        line, step = lines[0:1], lines[1:2]
        value = code[d, rows, :].astype(jnp.int32).astype(jnp.float32) * step
        own[d, rows, :] = own[d, rows, :] + value * upright(line)
        own[d, extra, :] = own[d, extra, :] + jnp.where(line_id == c, line, 0.0)

    def visit(p, carry):
        half = p // 2
        d = jnp.where(lax.rem(p, 2) == 0, length - 1 - half, half)
        partial(d * 2 + 1 - core, sib_out, d)
        sib_copy(d).start()
        partial(d * 2 + core, own, d)
        sib_copy(d).wait()
        own[d] = own[d] + sib_in[d]

        @pl.when((z == 0) & (d > 0))
        def _():
            for c in range(pairs):
                emit(True, d, c)

        @pl.when((z == length - 1) & (d < z))
        def _():
            for c in range(pairs):
                emit(False, d, c)

        return carry

    lax.fori_loop(0, length, visit, 0)

    def forward(index, carry):
        s, c = index // pairs, lax.rem(index, pairs)
        d, e = length - 1 - s, s

        @pl.when((z > 0) & (d >= z))
        def _():
            absorb(True, d, c)

            @pl.when(d > z)
            def _():
                emit(True, d, c)

        @pl.when((z < length - 1) & (e <= z))
        def _():
            absorb(False, e, c)

            @pl.when(e < z)
            def _():
                emit(False, e, c)

        return carry

    lax.fori_loop(0, length * pairs, forward, 0)
    gram[...] = jnp.zeros_like(gram)

    def finish(c, carry):
        where = pl.ds(pl.multiple_of(c * 256, 256), 256)
        image = own[z, where, :] / upright(totals_line(z, c))
        image_ref[where, :] = image
        gram[...] += lax.dot_general(image, image, (((0,), (0,)), ((), ())), precision=HIGHEST,
                                     preferred_element_type=jnp.float32)
        return carry

    lax.fori_loop(0, pairs, finish, 0)

    my_half = pl.ds(pl.multiple_of(core * 128, 128), 128)
    other_half = pl.ds(pl.multiple_of(128 - core * 128, 128), 128)
    halves = pltpu.make_async_remote_copy(
        src_ref=gram.at[other_half], dst_ref=gram_sib, send_sem=half_sem.at[0], recv_sem=half_sem.at[1],
        device_id={"rows": sibling}, device_id_type=MESH)
    halves.start()
    halves.wait()
    gram_half[...] = gram[my_half, :] + gram_sib[...]

    def piece_of(base, number):
        return pl.ds(pl.multiple_of(base + number * piece, piece), piece)

    sums = []
    for step in range(1, length):
        peer = lax.rem(z + step, length)
        sums.append(pltpu.make_async_remote_copy(
            src_ref=gram_half.at[piece_of(0, peer)], dst_ref=gram_z.at[z], send_sem=sum_send.at[step],
            recv_sem=sum_recv.at[step], device_id={"rows": peer * 2 + core}, device_id_type=MESH))
        sums[-1].start()
    total = gram_half[piece_of(0, z), :]
    for copy in sums:
        copy.wait()
    for step in range(1, length):
        total = total + gram_z[lax.rem(z + step, length)]
    gram_cols[col] = total
    crossings = []
    for step in range(1, n_cols):
        crossings.append(pltpu.make_async_remote_copy(
            src_ref=gram_cols.at[col], dst_ref=gram_cols.at[col], send_sem=col_send.at[step],
            recv_sem=col_recv.at[step], device_id={"cols": lax.rem(col + step, n_cols)}, device_id_type=MESH))
        crossings[-1].start()
    for copy in crossings:
        copy.wait()
    total = gram_cols[0]
    for number in range(1, n_cols):
        total = total + gram_cols[number]
    place = piece_of(core * 128, z)
    gram_all[place, :] = total
    backs = []
    for step in range(1, length):
        peer = lax.rem(z + step, length)
        backs.append(pltpu.make_async_remote_copy(
            src_ref=gram_all.at[place], dst_ref=gram_all.at[place], send_sem=back_send.at[step],
            recv_sem=back_recv.at[step], device_id={"rows": peer * 2 + core}, device_id_type=MESH))
        backs[-1].start()
    for copy in backs:
        copy.wait()
    last = pltpu.make_async_remote_copy(
        src_ref=gram_all.at[my_half], dst_ref=gram_all.at[my_half], send_sem=half_sem.at[2],
        recv_sem=half_sem.at[3], device_id={"rows": sibling}, device_id_type=MESH)
    last.start()
    last.wait()
    gram_ref[...] = gram_all[...]

    def settle(index, carry):
        d, c = index // pairs, lax.rem(index, pairs)

        @pl.when((z < length - 1) & (d > z))
        def _():
            for copy in chain_copies(True, d, c):
                copy.wait_send()

        @pl.when((z > 0) & (d < z))
        def _():
            for copy in chain_copies(False, d, c):
                copy.wait_send()

        return carry

    lax.fori_loop(0, length * pairs, settle, 0)


def factor(scale, gram_ref, image_ref, out_ref, work):
    size = SKETCH
    work[:, :size] = gram_ref[...]
    work[:, size:] = (lax.broadcasted_iota(jnp.int32, (size, size), 0)
                      == lax.broadcasted_iota(jnp.int32, (size, size), 1)).astype(jnp.float32)
    row_id = lax.broadcasted_iota(jnp.int32, (PANEL, 1), 0)
    for k in range(size // PANEL):
        first = k * PANEL
        panel = work[first:first + PANEL, :]
        for j in range(PANEL):
            at = first + j
            column = panel[:, at:at + 1]
            inverse = lax.rsqrt(panel[j:j + 1, at:at + 1])
            line = panel[j:j + 1, :] * inverse
            weight = jnp.where(row_id > j, column * inverse, 0.0)
            panel = jnp.where(row_id == j, line, panel - weight * line)
        work[first:first + PANEL, :] = panel
        after = first + PANEL
        if after < size:
            work[after:, :] -= lax.dot_general(
                panel[:, :size], panel, (((0,), (0,)), ((), ())), precision=HIGHEST,
                preferred_element_type=jnp.float32)[after:, :]
    lower = work[:, size:] * scale
    out_ref[...] = lax.dot_general(image_ref[...], lower, (((1,), (1,)), ((), ())), precision=HIGHEST,
                                   preferred_element_type=jnp.float32)


def per_device(tile_values, sketch, tile_coords, tile_counts):
    n_rows = lax.axis_size("rows")
    n_cols = lax.axis_size("cols")
    slots = tile_values.shape[2]
    depth = sketch.shape[0] * n_cols
    col_tiles = depth // TILE_SIZE
    row_tiles = col_tiles * n_rows // n_cols
    share = row_tiles * TILE_SIZE // n_rows
    length = n_rows // 2
    slot = jnp.arange(slots, dtype=jnp.int32)
    place = jnp.where(slot < tile_counts[0, 0], tile_coords[0, 0, 0] * col_tiles + tile_coords[0, 0, 1], -1)
    places = jnp.arange(row_tiles * col_tiles, dtype=jnp.int32)
    where = jnp.min(jnp.where(places[:, None] == place[None, :], slot[None, :], slots), axis=1)
    f32, vmem = jnp.float32, pltpu.VMEM
    dma = pltpu.SemaphoreType.DMA
    image, gram = pl.pallas_call(
        functools.partial(spread, n_rows, n_cols, slots, share, col_tiles),
        out_shape=(jax.ShapeDtypeStruct((share, SKETCH), f32), jax.ShapeDtypeStruct((SKETCH, SKETCH), f32)),
        in_specs=[pl.BlockSpec(memory_space=pltpu.SMEM), pl.BlockSpec(memory_space=pl.ANY),
                  pl.BlockSpec(memory_space=pl.ANY)],
        out_specs=(pl.BlockSpec(memory_space=vmem), pl.BlockSpec(memory_space=vmem)),
        scratch_shapes=[
            vmem((slots + 1, TILE_SIZE, TILE_SIZE), jnp.bfloat16),
            vmem((depth, SKETCH), jnp.bfloat16),
            vmem((256, depth), jnp.bfloat16),
        ] + [vmem((length, share + EXTRA, SKETCH), f32)] * 3 + [vmem((length, share, SKETCH), jnp.int16)] * 3 + [
            vmem((length, share // 32, SKETCH), f32)] * 3 + [
            vmem((SKETCH, SKETCH), f32), vmem((128, SKETCH), f32), vmem((128, SKETCH), f32),
            vmem((length, 128 // length, SKETCH), f32), vmem((n_cols, 128 // length, SKETCH), f32),
            vmem((SKETCH, SKETCH), f32),
            dma, dma, dma((n_cols,)), dma((n_cols,)), dma((length,)), dma((length,)),
        ] + [dma((length, share // 256, 2))] * 4 + [
            dma((4,)), dma((length,)), dma((length,)), dma((n_cols,)), dma((n_cols,)), dma((length,)), dma((length,))],
        compiler_params=pltpu.CompilerParams(collective_id=0, has_side_effects=True,
                                             vmem_limit_bytes=56 * 1024 * 1024),
    )(where, tile_values.reshape(slots, TILE_SIZE, TILE_SIZE), sketch)
    scale = math.sqrt(float(row_tiles * TILE_SIZE * n_cols))
    return pl.pallas_call(
        functools.partial(factor, scale),
        out_shape=jax.ShapeDtypeStruct((share, SKETCH), f32),
        in_specs=[pl.BlockSpec(memory_space=vmem)] * 2,
        out_specs=pl.BlockSpec(memory_space=vmem),
        scratch_shapes=[vmem((SKETCH, 2 * SKETCH), f32)],
        compiler_params=pltpu.CompilerParams(vmem_limit_bytes=32 * 1024 * 1024),
    )(gram, image)


def solution(mesh):
    return jax.shard_map(
        per_device,
        mesh=mesh,
        in_specs=(
            P(("groups", "rows"), "cols", None, None, None),
            P(("groups", "rows", "cols"), None),
            P(("groups", "rows"), "cols", None, None),
            P(("groups", "rows"), "cols"),
        ),
        out_specs=P(("groups", "cols", "rows"), None),
        check_vma=False,
    )
```

```python
import functools
import math

import jax
import jax.numpy as jnp
from jax import lax
from jax.experimental import pallas as pl
from jax.experimental.pallas import tpu as pltpu
from jax.sharding import PartitionSpec as P

TILE_SIZE = 128
SKETCH = 256
MESH = pl.DeviceIdType.MESH
EXTRA = 8
PANEL = 32
HIGHEST = lax.Precision.HIGHEST


def aligned(number, unit):
    return number * unit if isinstance(number, int) else pl.multiple_of(number * unit, unit)


def spread(n_rows, n_cols, slots, share, col_tiles, map_ref, tiles_hbm, sketch_hbm, image_ref, gram_ref,
           tiles, block, pair, own, sib_out, sib_in, code_out, code_left, code_right, side_out, side_left, side_right,
           gram, gram_sib, gram_half, gram_z, gram_cols, gram_all,
           tile_sem, local_sem, sk_send, sk_recv, sib_send, sib_recv,
           right_send, right_recv, left_send, left_recv,
           half_sem, sum_send, sum_recv, col_send, col_recv, back_send, back_recv):
    length = n_rows // 2
    part = block.shape[0] // n_cols
    pairs = share // 256
    piece = 128 // length
    me = lax.axis_index("rows")
    col = lax.axis_index("cols")
    z = me // 2
    core = lax.rem(me, 2)
    sibling = z * 2 + 1 - core

    tile_copy = pltpu.make_async_copy(tiles_hbm, tiles.at[pl.ds(0, slots)], tile_sem)
    tile_copy.start()
    mine = pl.ds(pl.multiple_of(col * part, part), part)
    sketch_copy = pltpu.make_async_copy(sketch_hbm, block.at[mine], local_sem)
    sketch_copy.start()

    barrier = pltpu.get_barrier_semaphore()
    pl.semaphore_signal(barrier, inc=1, device_id={"rows": sibling}, device_id_type=MESH)
    for step in range(1, n_cols):
        peer = lax.rem(col + step, n_cols)
        pl.semaphore_signal(barrier, inc=1, device_id={"cols": peer}, device_id_type=MESH)

    for step in range(1, length):
        peer = lax.rem(z + step, length) * 2 + core
        pl.semaphore_signal(barrier, inc=1, device_id={"rows": peer}, device_id_type=MESH)
    pl.semaphore_wait(barrier, n_cols + length - 1)

    def sketch_send(step):
        peer = lax.rem(col + step, n_cols)
        return pltpu.make_async_remote_copy(
            src_ref=sketch_hbm, dst_ref=block.at[mine], send_sem=sk_send.at[step], recv_sem=sk_recv.at[step],
            device_id={"cols": peer}, device_id_type=MESH)

    for step in range(1, n_cols):
        sketch_send(step).start()
    tiles[slots] = jnp.zeros((TILE_SIZE, TILE_SIZE), jnp.bfloat16)
    tile_copy.wait()
    sketch_copy.wait()
    for step in range(1, n_cols):
        sketch_send(step).wait()

    ones = jnp.ones((EXTRA, TILE_SIZE), jnp.float32)
    extra_id = lax.broadcasted_iota(jnp.int32, (EXTRA, TILE_SIZE), 0)

    def partial(number, dst, where):
        dst[where, pl.ds(share, EXTRA), :] = jnp.zeros((EXTRA, SKETCH), jnp.float32)

        def one(index, carry):
            for half in range(2):
                base = ((number * pairs + index) * 2 + half) * col_tiles
                total = jnp.zeros((TILE_SIZE, TILE_SIZE), jnp.float32)
                for c in range(col_tiles):
                    slab = tiles[map_ref[base + c]]
                    pair[half * TILE_SIZE:(half + 1) * TILE_SIZE, c * TILE_SIZE:(c + 1) * TILE_SIZE] = slab
                    total = total + slab.astype(jnp.float32)
                sums = lax.dot_general(ones, total, (((1,), (1,)), ((), ())), precision=HIGHEST,
                                       preferred_element_type=jnp.float32)
                lanes = slice(half * TILE_SIZE, (half + 1) * TILE_SIZE)
                kept = dst[where, pl.ds(share, EXTRA), lanes]
                dst[where, pl.ds(share, EXTRA), lanes] = jnp.where(extra_id == index, sums, kept)
            dst[where, pl.ds(pl.multiple_of(index * 256, 256), 256), :] = jnp.dot(
                pair[...], block[...], preferred_element_type=jnp.float32)
            return carry

        lax.fori_loop(0, pairs, one, 0)

    def sib_copy(d):
        return pltpu.make_async_remote_copy(
            src_ref=sib_out.at[d], dst_ref=sib_in.at[d], send_sem=sib_send.at[d], recv_sem=sib_recv.at[d],
            device_id={"rows": sibling}, device_id_type=MESH)

    def chain_copies(to_right, d, c):
        rows, lines = pl.ds(aligned(c, 256), 256), pl.ds(aligned(c, 8), 8)
        code, side = (code_left, side_left) if to_right else (code_right, side_right)
        send, recv = (right_send, right_recv) if to_right else (left_send, left_recv)
        peer = me + 2 if to_right else me - 2
        return (
            pltpu.make_async_remote_copy(
                src_ref=code_out.at[d, rows], dst_ref=code.at[d, rows], send_sem=send.at[d, c, 0],
                recv_sem=recv.at[d, c, 0], device_id={"rows": peer}, device_id_type=MESH),
            pltpu.make_async_remote_copy(
                src_ref=side_out.at[d, lines], dst_ref=side.at[d, lines], send_sem=send.at[d, c, 1],
                recv_sem=recv.at[d, c, 1], device_id={"rows": peer}, device_id_type=MESH),
        )

    eye = lax.broadcasted_iota(jnp.int32, (256, 256), 0) == lax.broadcasted_iota(jnp.int32, (256, 256), 1)
    line_id = lax.broadcasted_iota(jnp.int32, (EXTRA, SKETCH), 0)

    def upright(line):
        return jnp.sum(jnp.where(eye, jnp.broadcast_to(line, (256, 256)), 0.0), axis=1, keepdims=True)

    def totals_line(d, c):
        return jnp.sum(jnp.where(line_id == c, own[d, pl.ds(share, EXTRA), :], 0.0), axis=0, keepdims=True)

    def emit(to_right, d, c):
        rows = pl.ds(aligned(c, 256), 256)
        line = totals_line(d, c)
        ratio = own[d, rows, :] * upright(1.0 / jnp.where(line > 0, line, 1.0))
        step = jnp.maximum(jnp.max(jnp.abs(ratio), axis=0, keepdims=True) * (1.0 / 32767.0), 1e-30)
        code_out[d, rows, :] = jnp.round(ratio * (1.0 / step)).astype(jnp.int32).astype(jnp.int16)
        side_out[d, pl.ds(aligned(c, 8), 8), :] = jnp.where(line_id == 0, line, step)
        for copy in chain_copies(to_right, d, c):
            copy.start()

    def absorb(to_right, d, c):
        for copy in chain_copies(to_right, d, c):
            copy.wait_recv()
        code, side = (code_left, side_left) if to_right else (code_right, side_right)
        rows, extra = pl.ds(aligned(c, 256), 256), pl.ds(share, EXTRA)
        lines = side[d, pl.ds(aligned(c, 8), 8), :]
        line, step = lines[0:1], lines[1:2]
        value = code[d, rows, :].astype(jnp.int32).astype(jnp.float32) * step
        own[d, rows, :] = own[d, rows, :] + value * upright(line)
        own[d, extra, :] = own[d, extra, :] + jnp.where(line_id == c, line, 0.0)

    def visit(p, carry):
        half = p // 2
        d = jnp.where(lax.rem(p, 2) == 0, length - 1 - half, half)
        partial(d * 2 + 1 - core, sib_out, d)
        sib_copy(d).start()
        partial(d * 2 + core, own, d)
        sib_copy(d).wait()
        own[d] = own[d] + sib_in[d]

        @pl.when((z == 0) & (d > 0))
        def _():
            for c in range(pairs):
                emit(True, d, c)

        @pl.when((z == length - 1) & (d < z))
        def _():
            for c in range(pairs):
                emit(False, d, c)

        return carry

    lax.fori_loop(0, length, visit, 0)

    chunks = length * pairs
    lag = pairs + 1

    def forward(index, carry):
        low = z < length // 2
        rightward = jnp.where(low, index, index - lag)
        leftward = jnp.where(low, index - lag, index)

        @pl.when((rightward >= 0) & (rightward < chunks))
        def _():
            d, c = length - 1 - rightward // pairs, lax.rem(rightward, pairs)

            @pl.when((z > 0) & (d >= z))
            def _():
                absorb(True, d, c)

                @pl.when(d > z)
                def _():
                    emit(True, d, c)

        @pl.when((leftward >= 0) & (leftward < chunks))
        def _():
            e, c = leftward // pairs, lax.rem(leftward, pairs)

            @pl.when((z < length - 1) & (e <= z))
            def _():
                absorb(False, e, c)

                @pl.when(e < z)
                def _():
                    emit(False, e, c)

        return carry

    lax.fori_loop(0, chunks + lag, forward, 0)
    gram[...] = jnp.zeros_like(gram)

    def finish(c, carry):
        where = pl.ds(pl.multiple_of(c * 256, 256), 256)
        image = own[z, where, :] / upright(totals_line(z, c))
        image_ref[where, :] = image
        gram[...] += lax.dot_general(image, image, (((0,), (0,)), ((), ())), precision=HIGHEST,
                                     preferred_element_type=jnp.float32)
        return carry

    lax.fori_loop(0, pairs, finish, 0)

    my_half = pl.ds(pl.multiple_of(core * 128, 128), 128)
    other_half = pl.ds(pl.multiple_of(128 - core * 128, 128), 128)
    halves = pltpu.make_async_remote_copy(
        src_ref=gram.at[other_half], dst_ref=gram_sib, send_sem=half_sem.at[0], recv_sem=half_sem.at[1],
        device_id={"rows": sibling}, device_id_type=MESH)
    halves.start()
    halves.wait()
    gram_half[...] = gram[my_half, :] + gram_sib[...]

    def piece_of(base, number):
        return pl.ds(pl.multiple_of(base + number * piece, piece), piece)

    sums = []
    for step in range(1, length):
        peer = lax.rem(z + step, length)
        sums.append(pltpu.make_async_remote_copy(
            src_ref=gram_half.at[piece_of(0, peer)], dst_ref=gram_z.at[z], send_sem=sum_send.at[step],
            recv_sem=sum_recv.at[step], device_id={"rows": peer * 2 + core}, device_id_type=MESH))
        sums[-1].start()
    total = gram_half[piece_of(0, z), :]
    for copy in sums:
        copy.wait()
    for step in range(1, length):
        total = total + gram_z[lax.rem(z + step, length)]
    gram_cols[col] = total
    crossings = []
    for step in range(1, n_cols):
        crossings.append(pltpu.make_async_remote_copy(
            src_ref=gram_cols.at[col], dst_ref=gram_cols.at[col], send_sem=col_send.at[step],
            recv_sem=col_recv.at[step], device_id={"cols": lax.rem(col + step, n_cols)}, device_id_type=MESH))
        crossings[-1].start()
    for copy in crossings:
        copy.wait()
    total = gram_cols[0]
    for number in range(1, n_cols):
        total = total + gram_cols[number]
    place = piece_of(core * 128, z)
    gram_all[place, :] = total
    backs = []
    for step in range(1, length):
        peer = lax.rem(z + step, length)
        backs.append(pltpu.make_async_remote_copy(
            src_ref=gram_all.at[place], dst_ref=gram_all.at[place], send_sem=back_send.at[step],
            recv_sem=back_recv.at[step], device_id={"rows": peer * 2 + core}, device_id_type=MESH))
        backs[-1].start()
    for copy in backs:
        copy.wait()
    last = pltpu.make_async_remote_copy(
        src_ref=gram_all.at[my_half], dst_ref=gram_all.at[my_half], send_sem=half_sem.at[2],
        recv_sem=half_sem.at[3], device_id={"rows": sibling}, device_id_type=MESH)
    last.start()
    last.wait()
    gram_ref[...] = gram_all[...]

    def settle(index, carry):
        d, c = index // pairs, lax.rem(index, pairs)

        @pl.when((z < length - 1) & (d > z))
        def _():
            for copy in chain_copies(True, d, c):
                copy.wait_send()

        @pl.when((z > 0) & (d < z))
        def _():
            for copy in chain_copies(False, d, c):
                copy.wait_send()

        return carry

    lax.fori_loop(0, length * pairs, settle, 0)


def factor(scale, gram_ref, image_ref, out_ref, work):
    size = SKETCH
    work[:, :size] = gram_ref[...]
    work[:, size:] = (lax.broadcasted_iota(jnp.int32, (size, size), 0)
                      == lax.broadcasted_iota(jnp.int32, (size, size), 1)).astype(jnp.float32)
    row_id = lax.broadcasted_iota(jnp.int32, (PANEL, 1), 0)
    lane_id = lax.broadcasted_iota(jnp.int32, (PANEL, size), 1)
    for k in range(size // PANEL):
        first = k * PANEL
        panel = work[first:first + PANEL, :]
        for j in range(0, PANEL, 2):
            at = first + j
            column, second = panel[:, at:at + 1], panel[:, at + 1:at + 2]
            inverse = 1.0 / column[j:j + 1]
            ratio = column[j + 1:j + 2] * inverse
            pivot = second[j + 1:j + 2] - column[j + 1:j + 2] * ratio
            line = panel[j:j + 1, :]
            below = panel[j + 1:j + 2, :] - ratio * line
            weight = jnp.where(row_id > j, column * inverse, 0.0)
            other = jnp.where(row_id > j + 1, (second - column * ratio) * (1.0 / pivot), 0.0)
            panel = panel - weight * line - other * below
        diagonal = jnp.sum(jnp.where(lane_id == first + row_id, panel[:, :size], 0.0), axis=1, keepdims=True)
        panel = panel * lax.rsqrt(diagonal)
        work[first:first + PANEL, :] = panel
        after = first + PANEL
        if after < size:
            work[after:, :] -= lax.dot_general(
                panel[:, :size], panel, (((0,), (0,)), ((), ())), precision=HIGHEST,
                preferred_element_type=jnp.float32)[after:, :]
    lower = work[:, size:] * scale
    out_ref[...] = lax.dot_general(image_ref[...], lower, (((1,), (1,)), ((), ())), precision=HIGHEST,
                                   preferred_element_type=jnp.float32)


def per_device(tile_values, sketch, tile_coords, tile_counts):
    n_rows = lax.axis_size("rows")
    n_cols = lax.axis_size("cols")
    slots = tile_values.shape[2]
    depth = sketch.shape[0] * n_cols
    col_tiles = depth // TILE_SIZE
    row_tiles = col_tiles * n_rows // n_cols
    share = row_tiles * TILE_SIZE // n_rows
    length = n_rows // 2
    slot = jnp.arange(slots, dtype=jnp.int32)
    place = jnp.where(slot < tile_counts[0, 0], tile_coords[0, 0, 0] * col_tiles + tile_coords[0, 0, 1], -1)
    places = jnp.arange(row_tiles * col_tiles, dtype=jnp.int32)
    where = jnp.min(jnp.where(places[:, None] == place[None, :], slot[None, :], slots), axis=1)
    f32, vmem = jnp.float32, pltpu.VMEM
    dma = pltpu.SemaphoreType.DMA
    image, gram = pl.pallas_call(
        functools.partial(spread, n_rows, n_cols, slots, share, col_tiles),
        out_shape=(jax.ShapeDtypeStruct((share, SKETCH), f32), jax.ShapeDtypeStruct((SKETCH, SKETCH), f32)),
        in_specs=[pl.BlockSpec(memory_space=pltpu.SMEM), pl.BlockSpec(memory_space=pl.ANY),
                  pl.BlockSpec(memory_space=pl.ANY)],
        out_specs=(pl.BlockSpec(memory_space=vmem), pl.BlockSpec(memory_space=vmem)),
        scratch_shapes=[
            vmem((slots + 1, TILE_SIZE, TILE_SIZE), jnp.bfloat16),
            vmem((depth, SKETCH), jnp.bfloat16),
            vmem((256, depth), jnp.bfloat16),
        ] + [vmem((length, share + EXTRA, SKETCH), f32)] * 3 + [vmem((length, share, SKETCH), jnp.int16)] * 3 + [
            vmem((length, share // 32, SKETCH), f32)] * 3 + [
            vmem((SKETCH, SKETCH), f32), vmem((128, SKETCH), f32), vmem((128, SKETCH), f32),
            vmem((length, 128 // length, SKETCH), f32), vmem((n_cols, 128 // length, SKETCH), f32),
            vmem((SKETCH, SKETCH), f32),
            dma, dma, dma((n_cols,)), dma((n_cols,)), dma((length,)), dma((length,)),
        ] + [dma((length, share // 256, 2))] * 4 + [
            dma((4,)), dma((length,)), dma((length,)), dma((n_cols,)), dma((n_cols,)), dma((length,)), dma((length,))],
        compiler_params=pltpu.CompilerParams(collective_id=0, has_side_effects=True,
                                             vmem_limit_bytes=56 * 1024 * 1024),
    )(where, tile_values.reshape(slots, TILE_SIZE, TILE_SIZE), sketch)
    scale = math.sqrt(float(row_tiles * TILE_SIZE * n_cols))
    return pl.pallas_call(
        functools.partial(factor, scale),
        out_shape=jax.ShapeDtypeStruct((share, SKETCH), f32),
        in_specs=[pl.BlockSpec(memory_space=vmem)] * 2,
        out_specs=pl.BlockSpec(memory_space=vmem),
        scratch_shapes=[vmem((SKETCH, 2 * SKETCH), f32)],
        compiler_params=pltpu.CompilerParams(vmem_limit_bytes=32 * 1024 * 1024),
    )(gram, image)


def solution(mesh):
    return jax.shard_map(
        per_device,
        mesh=mesh,
        in_specs=(
            P(("groups", "rows"), "cols", None, None, None),
            P(("groups", "rows", "cols"), None),
            P(("groups", "rows"), "cols", None, None),
            P(("groups", "rows"), "cols"),
        ),
        out_specs=P(("groups", "cols", "rows"), None),
        check_vma=False,
    )
```

```python
import functools
import math

import jax
import jax.numpy as jnp
from jax import lax
from jax.experimental import pallas as pl
from jax.experimental.pallas import tpu as pltpu
from jax.sharding import PartitionSpec as P

TILE_SIZE = 128
SKETCH = 256
MESH = pl.DeviceIdType.MESH
EXTRA = 8
PANEL = 64
HIGHEST = lax.Precision.HIGHEST


def aligned(number, unit):
    return number * unit if isinstance(number, int) else pl.multiple_of(number * unit, unit)


def spread(n_rows, n_cols, slots, share, col_tiles, map_ref, tiles_hbm, sketch_hbm, image_ref, gram_ref,
           tiles, block, pair, own, sib_out, sib_in, code_out, code_left, code_right, side_out, side_left, side_right,
           gram, gram_sib, gram_half, gram_z, gram_cols, gram_all,
           tile_sem, local_sem, sk_send, sk_recv, sib_send, sib_recv,
           right_send, right_recv, left_send, left_recv,
           half_sem, sum_send, sum_recv, col_send, col_recv, back_send, back_recv):
    length = n_rows // 2
    part = block.shape[0] // n_cols
    pairs = share // 256
    piece = 128 // length
    me = lax.axis_index("rows")
    col = lax.axis_index("cols")
    z = me // 2
    core = lax.rem(me, 2)
    sibling = z * 2 + 1 - core

    tile_copy = pltpu.make_async_copy(tiles_hbm, tiles.at[pl.ds(0, slots)], tile_sem)
    tile_copy.start()
    mine = pl.ds(pl.multiple_of(col * part, part), part)
    sketch_copy = pltpu.make_async_copy(sketch_hbm, block.at[mine], local_sem)
    sketch_copy.start()

    barrier = pltpu.get_barrier_semaphore()
    pl.semaphore_signal(barrier, inc=1, device_id={"rows": sibling}, device_id_type=MESH)
    for step in range(1, n_cols):
        peer = lax.rem(col + step, n_cols)
        pl.semaphore_signal(barrier, inc=1, device_id={"cols": peer}, device_id_type=MESH)

    for step in range(1, length):
        peer = lax.rem(z + step, length) * 2 + core
        pl.semaphore_signal(barrier, inc=1, device_id={"rows": peer}, device_id_type=MESH)
    pl.semaphore_wait(barrier, n_cols + length - 1)

    def sketch_send(step):
        peer = lax.rem(col + step, n_cols)
        return pltpu.make_async_remote_copy(
            src_ref=sketch_hbm, dst_ref=block.at[mine], send_sem=sk_send.at[step], recv_sem=sk_recv.at[step],
            device_id={"cols": peer}, device_id_type=MESH)

    for step in range(1, n_cols):
        sketch_send(step).start()
    tiles[slots] = jnp.zeros((TILE_SIZE, TILE_SIZE), jnp.bfloat16)
    tile_copy.wait()
    sketch_copy.wait()
    for step in range(1, n_cols):
        sketch_send(step).wait()

    ones = jnp.ones((EXTRA, TILE_SIZE), jnp.float32)
    extra_id = lax.broadcasted_iota(jnp.int32, (EXTRA, TILE_SIZE), 0)

    def partial(number, dst, where):
        dst[where, pl.ds(share, EXTRA), :] = jnp.zeros((EXTRA, SKETCH), jnp.float32)

        def one(index, carry):
            for half in range(2):
                base = ((number * pairs + index) * 2 + half) * col_tiles
                total = jnp.zeros((TILE_SIZE, TILE_SIZE), jnp.float32)
                for c in range(col_tiles):
                    slab = tiles[map_ref[base + c]]
                    pair[half * TILE_SIZE:(half + 1) * TILE_SIZE, c * TILE_SIZE:(c + 1) * TILE_SIZE] = slab
                    total = total + slab.astype(jnp.float32)
                sums = lax.dot_general(ones, total, (((1,), (1,)), ((), ())), precision=HIGHEST,
                                       preferred_element_type=jnp.float32)
                lanes = slice(half * TILE_SIZE, (half + 1) * TILE_SIZE)
                kept = dst[where, pl.ds(share, EXTRA), lanes]
                dst[where, pl.ds(share, EXTRA), lanes] = jnp.where(extra_id == index, sums, kept)
            dst[where, pl.ds(pl.multiple_of(index * 256, 256), 256), :] = jnp.dot(
                pair[...], block[...], preferred_element_type=jnp.float32)
            return carry

        lax.fori_loop(0, pairs, one, 0)

    def sib_copy(d):
        return pltpu.make_async_remote_copy(
            src_ref=sib_out.at[d], dst_ref=sib_in.at[d], send_sem=sib_send.at[d], recv_sem=sib_recv.at[d],
            device_id={"rows": sibling}, device_id_type=MESH)

    def chain_copies(to_right, d, c):
        rows, lines = pl.ds(aligned(c, 256), 256), pl.ds(aligned(c, 8), 8)
        code, side = (code_left, side_left) if to_right else (code_right, side_right)
        send, recv = (right_send, right_recv) if to_right else (left_send, left_recv)
        peer = me + 2 if to_right else me - 2
        return (
            pltpu.make_async_remote_copy(
                src_ref=code_out.at[d, rows], dst_ref=code.at[d, rows], send_sem=send.at[d, c, 0],
                recv_sem=recv.at[d, c, 0], device_id={"rows": peer}, device_id_type=MESH),
            pltpu.make_async_remote_copy(
                src_ref=side_out.at[d, lines], dst_ref=side.at[d, lines], send_sem=send.at[d, c, 1],
                recv_sem=recv.at[d, c, 1], device_id={"rows": peer}, device_id_type=MESH),
        )

    eye = lax.broadcasted_iota(jnp.int32, (256, 256), 0) == lax.broadcasted_iota(jnp.int32, (256, 256), 1)
    line_id = lax.broadcasted_iota(jnp.int32, (EXTRA, SKETCH), 0)

    def upright(line):
        return jnp.sum(jnp.where(eye, jnp.broadcast_to(line, (256, 256)), 0.0), axis=1, keepdims=True)

    def totals_line(d, c):
        return jnp.sum(jnp.where(line_id == c, own[d, pl.ds(share, EXTRA), :], 0.0), axis=0, keepdims=True)

    def emit(to_right, d, c):
        rows = pl.ds(aligned(c, 256), 256)
        line = totals_line(d, c)
        ratio = own[d, rows, :] * upright(1.0 / jnp.where(line > 0, line, 1.0))
        step = jnp.maximum(jnp.max(jnp.abs(ratio), axis=0, keepdims=True) * (1.0 / 32767.0), 1e-30)
        code_out[d, rows, :] = jnp.round(ratio * (1.0 / step)).astype(jnp.int32).astype(jnp.int16)
        side_out[d, pl.ds(aligned(c, 8), 8), :] = jnp.where(line_id == 0, line, step)
        for copy in chain_copies(to_right, d, c):
            copy.start()

    def absorb(to_right, d, c):
        for copy in chain_copies(to_right, d, c):
            copy.wait_recv()
        code, side = (code_left, side_left) if to_right else (code_right, side_right)
        rows, extra = pl.ds(aligned(c, 256), 256), pl.ds(share, EXTRA)
        lines = side[d, pl.ds(aligned(c, 8), 8), :]
        line, step = lines[0:1], lines[1:2]
        value = code[d, rows, :].astype(jnp.int32).astype(jnp.float32) * step
        own[d, rows, :] = own[d, rows, :] + value * upright(line)
        own[d, extra, :] = own[d, extra, :] + jnp.where(line_id == c, line, 0.0)

    def visit(p, carry):
        half = p // 2
        d = jnp.where(lax.rem(p, 2) == 0, length - 1 - half, half)
        partial(d * 2 + 1 - core, sib_out, d)
        sib_copy(d).start()
        partial(d * 2 + core, own, d)
        sib_copy(d).wait()
        own[d] = own[d] + sib_in[d]

        @pl.when((z == 0) & (d > 0))
        def _():
            for c in range(pairs):
                emit(True, d, c)

        @pl.when((z == length - 1) & (d < z))
        def _():
            for c in range(pairs):
                emit(False, d, c)

        return carry

    lax.fori_loop(0, length, visit, 0)

    chunks = length * pairs
    lag = pairs + 1

    def forward(index, carry):
        low = z < length // 2
        rightward = jnp.where(low, index, index - lag)
        leftward = jnp.where(low, index - lag, index)

        @pl.when((rightward >= 0) & (rightward < chunks))
        def _():
            d, c = length - 1 - rightward // pairs, lax.rem(rightward, pairs)

            @pl.when((z > 0) & (d >= z))
            def _():
                absorb(True, d, c)

                @pl.when(d > z)
                def _():
                    emit(True, d, c)

        @pl.when((leftward >= 0) & (leftward < chunks))
        def _():
            e, c = leftward // pairs, lax.rem(leftward, pairs)

            @pl.when((z < length - 1) & (e <= z))
            def _():
                absorb(False, e, c)

                @pl.when(e < z)
                def _():
                    emit(False, e, c)

        return carry

    lax.fori_loop(0, chunks + lag, forward, 0)
    gram[...] = jnp.zeros_like(gram)

    def finish(c, carry):
        where = pl.ds(pl.multiple_of(c * 256, 256), 256)
        image = own[z, where, :] / upright(totals_line(z, c))
        image_ref[where, :] = image
        gram[...] += lax.dot_general(image, image, (((0,), (0,)), ((), ())), precision=HIGHEST,
                                     preferred_element_type=jnp.float32)
        return carry

    lax.fori_loop(0, pairs, finish, 0)

    my_half = pl.ds(pl.multiple_of(core * 128, 128), 128)
    other_half = pl.ds(pl.multiple_of(128 - core * 128, 128), 128)
    halves = pltpu.make_async_remote_copy(
        src_ref=gram.at[other_half], dst_ref=gram_sib, send_sem=half_sem.at[0], recv_sem=half_sem.at[1],
        device_id={"rows": sibling}, device_id_type=MESH)
    halves.start()
    halves.wait()
    gram_half[...] = gram[my_half, :] + gram_sib[...]

    def piece_of(base, number):
        return pl.ds(pl.multiple_of(base + number * piece, piece), piece)

    sums = []
    for step in range(1, length):
        peer = lax.rem(z + step, length)
        sums.append(pltpu.make_async_remote_copy(
            src_ref=gram_half.at[piece_of(0, peer)], dst_ref=gram_z.at[z], send_sem=sum_send.at[step],
            recv_sem=sum_recv.at[step], device_id={"rows": peer * 2 + core}, device_id_type=MESH))
        sums[-1].start()
    total = gram_half[piece_of(0, z), :]
    for copy in sums:
        copy.wait()
    for step in range(1, length):
        total = total + gram_z[lax.rem(z + step, length)]
    gram_cols[col] = total
    crossings = []
    for step in range(1, n_cols):
        crossings.append(pltpu.make_async_remote_copy(
            src_ref=gram_cols.at[col], dst_ref=gram_cols.at[col], send_sem=col_send.at[step],
            recv_sem=col_recv.at[step], device_id={"cols": lax.rem(col + step, n_cols)}, device_id_type=MESH))
        crossings[-1].start()
    for copy in crossings:
        copy.wait()
    total = gram_cols[0]
    for number in range(1, n_cols):
        total = total + gram_cols[number]
    place = piece_of(core * 128, z)
    gram_all[place, :] = total
    backs = []
    for step in range(1, length):
        peer = lax.rem(z + step, length)
        backs.append(pltpu.make_async_remote_copy(
            src_ref=gram_all.at[place], dst_ref=gram_all.at[place], send_sem=back_send.at[step],
            recv_sem=back_recv.at[step], device_id={"rows": peer * 2 + core}, device_id_type=MESH))
        backs[-1].start()
    for copy in backs:
        copy.wait()
    last = pltpu.make_async_remote_copy(
        src_ref=gram_all.at[my_half], dst_ref=gram_all.at[my_half], send_sem=half_sem.at[2],
        recv_sem=half_sem.at[3], device_id={"rows": sibling}, device_id_type=MESH)
    last.start()
    last.wait()
    gram_ref[...] = gram_all[...]

    def settle(index, carry):
        d, c = index // pairs, lax.rem(index, pairs)

        @pl.when((z < length - 1) & (d > z))
        def _():
            for copy in chain_copies(True, d, c):
                copy.wait_send()

        @pl.when((z > 0) & (d < z))
        def _():
            for copy in chain_copies(False, d, c):
                copy.wait_send()

        return carry

    lax.fori_loop(0, length * pairs, settle, 0)


def factor(scale, gram_ref, image_ref, out_ref, work):
    size = SKETCH
    work[:, :size] = gram_ref[...]
    work[:, size:] = (lax.broadcasted_iota(jnp.int32, (size, size), 0)
                      == lax.broadcasted_iota(jnp.int32, (size, size), 1)).astype(jnp.float32)
    row_id = lax.broadcasted_iota(jnp.int32, (PANEL, 1), 0)
    lane_id = lax.broadcasted_iota(jnp.int32, (PANEL, size), 1)
    for k in range(size // PANEL):
        first = k * PANEL
        panel = work[first:first + PANEL, :]
        for j in range(0, PANEL, 2):
            at = first + j
            column, second = panel[:, at:at + 1], panel[:, at + 1:at + 2]
            inverse = 1.0 / column[j:j + 1]
            ratio = column[j + 1:j + 2] * inverse
            pivot = second[j + 1:j + 2] - column[j + 1:j + 2] * ratio
            line = panel[j:j + 1, :]
            below = panel[j + 1:j + 2, :] - ratio * line
            weight = jnp.where(row_id > j, column * inverse, 0.0)
            other = jnp.where(row_id > j + 1, (second - column * ratio) * (1.0 / pivot), 0.0)
            panel = panel - weight * line - other * below
        diagonal = jnp.sum(jnp.where(lane_id == first + row_id, panel[:, :size], 0.0), axis=1, keepdims=True)
        panel = panel * lax.rsqrt(diagonal)
        work[first:first + PANEL, :] = panel
        after = first + PANEL
        if after < size:
            lo, hi = after // 128 * 128, size + (after + 127) // 128 * 128
            work[after:, lo:hi] -= lax.dot_general(
                panel[:, lo:size], panel[:, lo:hi], (((0,), (0,)), ((), ())), precision=HIGHEST,
                preferred_element_type=jnp.float32)[after - lo:, :]
    lower = work[:, size:] * scale
    out_ref[...] = lax.dot_general(image_ref[...], lower, (((1,), (1,)), ((), ())), precision=HIGHEST,
                                   preferred_element_type=jnp.float32)


def per_device(tile_values, sketch, tile_coords, tile_counts):
    n_rows = lax.axis_size("rows")
    n_cols = lax.axis_size("cols")
    slots = tile_values.shape[2]
    depth = sketch.shape[0] * n_cols
    col_tiles = depth // TILE_SIZE
    row_tiles = col_tiles * n_rows // n_cols
    share = row_tiles * TILE_SIZE // n_rows
    length = n_rows // 2
    slot = jnp.arange(slots, dtype=jnp.int32)
    place = jnp.where(slot < tile_counts[0, 0], tile_coords[0, 0, 0] * col_tiles + tile_coords[0, 0, 1], -1)
    places = jnp.arange(row_tiles * col_tiles, dtype=jnp.int32)
    where = jnp.min(jnp.where(places[:, None] == place[None, :], slot[None, :], slots), axis=1)
    f32, vmem = jnp.float32, pltpu.VMEM
    dma = pltpu.SemaphoreType.DMA
    image, gram = pl.pallas_call(
        functools.partial(spread, n_rows, n_cols, slots, share, col_tiles),
        out_shape=(jax.ShapeDtypeStruct((share, SKETCH), f32), jax.ShapeDtypeStruct((SKETCH, SKETCH), f32)),
        in_specs=[pl.BlockSpec(memory_space=pltpu.SMEM), pl.BlockSpec(memory_space=pl.ANY),
                  pl.BlockSpec(memory_space=pl.ANY)],
        out_specs=(pl.BlockSpec(memory_space=vmem), pl.BlockSpec(memory_space=vmem)),
        scratch_shapes=[
            vmem((slots + 1, TILE_SIZE, TILE_SIZE), jnp.bfloat16),
            vmem((depth, SKETCH), jnp.bfloat16),
            vmem((256, depth), jnp.bfloat16),
        ] + [vmem((length, share + EXTRA, SKETCH), f32)] * 3 + [vmem((length, share, SKETCH), jnp.int16)] * 3 + [
            vmem((length, share // 32, SKETCH), f32)] * 3 + [
            vmem((SKETCH, SKETCH), f32), vmem((128, SKETCH), f32), vmem((128, SKETCH), f32),
            vmem((length, 128 // length, SKETCH), f32), vmem((n_cols, 128 // length, SKETCH), f32),
            vmem((SKETCH, SKETCH), f32),
            dma, dma, dma((n_cols,)), dma((n_cols,)), dma((length,)), dma((length,)),
        ] + [dma((length, share // 256, 2))] * 4 + [
            dma((4,)), dma((length,)), dma((length,)), dma((n_cols,)), dma((n_cols,)), dma((length,)), dma((length,))],
        compiler_params=pltpu.CompilerParams(collective_id=0, has_side_effects=True,
                                             vmem_limit_bytes=56 * 1024 * 1024),
    )(where, tile_values.reshape(slots, TILE_SIZE, TILE_SIZE), sketch)
    scale = math.sqrt(float(row_tiles * TILE_SIZE * n_cols))
    return pl.pallas_call(
        functools.partial(factor, scale),
        out_shape=jax.ShapeDtypeStruct((share, SKETCH), f32),
        in_specs=[pl.BlockSpec(memory_space=vmem)] * 2,
        out_specs=pl.BlockSpec(memory_space=vmem),
        scratch_shapes=[vmem((SKETCH, 2 * SKETCH), f32)],
        compiler_params=pltpu.CompilerParams(vmem_limit_bytes=32 * 1024 * 1024),
    )(gram, image)


def solution(mesh):
    return jax.shard_map(
        per_device,
        mesh=mesh,
        in_specs=(
            P(("groups", "rows"), "cols", None, None, None),
            P(("groups", "rows", "cols"), None),
            P(("groups", "rows"), "cols", None, None),
            P(("groups", "rows"), "cols"),
        ),
        out_specs=P(("groups", "cols", "rows"), None),
        check_vma=False,
    )
```
